512 devices in a mesh: tile: 64 (over y_lo, z, x), head: 8 (over y_hi, core).
Axes of the slice: x: 4, y: 8 (y_hi: 4, y_lo: 2; y = y_hi * 2 + y_lo), z: 8, core: 2. Of those that a mesh axis runs over, the one named last changes fastest.
Arguments:
- q_video: bfloat16 [49152, 3072], P('tile', 'head'), may hold values from -12 to 12
- k_video: bfloat16 [49152, 3072], P('tile', 'head'), may hold values from -12 to 12
- v_video: bfloat16 [49152, 3072], P('tile', 'head'), may hold values from -6 to 6
- q_text: bfloat16 [256, 3072], P('tile', 'head'), may hold values from -12 to 12
- k_text: bfloat16 [256, 3072], P('tile', 'head'), may hold values from -6 to 6
- v_text: bfloat16 [256, 3072], P('tile', 'head'), may hold values from -6 to 6
- tile_lists: int32 [128, 8], P('tile'), may hold values from -1 to 127, as said below
- text_len: int32 [1], replicated, may hold values from 64 to 256
Outputs:
- video_out: bfloat16 [49152, 3072], P(('tile', 'head'))
- text_out: bfloat16 [256, 3072], P('tile', 'head')
The draws below stay inside these ranges and needn't reach their ends.
Inputs may be any that keep to these rules, and one draw needn't show every extreme that they name: `tile_lists`: row g lists key tiles for video tile g, whose time, height and width tile coordinates are g % 2, (g // 2) // 8 and (g // 2) % 8; a tile's number is ((height * 8) + width) * 2 + time. The first entry is g itself, the next entries are distinct tiles whose three coordinates each differ from g's by at most one, and -1 fills the empty slots at the end. Some row is full.
All inputs are finite; a program needn't handle non-finite values.
Results may differ from the reference program's by a relative error of at most 0.0054.
Values may be sent and summed in bfloat16 or wider, within the bound.
No kernel may reach another device: no remote copies, remote signals or barrier semaphores. Data moves between devices by JAX's collectives and lax.ppermute only.
A program may use at most 128 MiB of HBM per device.

```python
import math
import jax
import jax.numpy as jnp
from jax import lax

HEADS = 24
HEAD_DIM = 128
TEXT = 256
TILE_TOK = 384
TILES_W = 8
TILES_T = 2
TILES_H = 8
TILES = 128
NB = 8
VIDEO = 49152
FEATURES = 3072


def common_signs(key):
    return jax.random.bernoulli(key, 0.5, (TILES, FEATURES)).astype(jnp.float32) * 2.0 - 1.0


def squared_levels():
    fraction = (jnp.arange(TILES) % 8).astype(jnp.float32) / 7.0
    return (110.0 + 220.0 * fraction) / HEAD_DIM ** 0.5


def strengths():
    return jnp.sqrt(squared_levels())


def base_draw(key, shape):
    return jax.random.truncated_normal(key, -4.5, 4.5, shape, jnp.float32)


def draw_q_video(key, part):
    signs = common_signs(key)
    key = jax.random.fold_in(key, 11)
    base = base_draw(key, (TILES, TILE_TOK, FEATURES))
    base = base.at[:, 0].set(strengths()[:, None] * signs)
    return base.reshape(VIDEO, FEATURES).astype(jnp.bfloat16)


def draw_k_video(key, part):
    signs = common_signs(key)
    key = jax.random.fold_in(key, 13)
    base = base_draw(key, (TILES, TILE_TOK, FEATURES))
    lifted = strengths()[:, None] * signs
    cut = 2.0 * HEAD_DIM ** 0.5 / squared_levels()
    leading = jnp.arange(FEATURES) % HEAD_DIM == 0
    factor = jnp.where(leading[None, :], 1.0 - cut[:, None], 1.0)
    base = base.at[:, 1].set(lifted)
    base = base.at[:, 2].set(lifted * factor)
    return base.reshape(VIDEO, FEATURES).astype(jnp.bfloat16)


def draw_q_text(key, part):
    signs = common_signs(key)
    key = jax.random.fold_in(key, 17)
    base = base_draw(key, (TEXT, FEATURES))
    count = min(TEXT, (TILES + 3) // 4)
    lifted = strengths()[::4][:count, None] * signs[::4][:count]
    base = base.at[:count].set(lifted)
    return base.astype(jnp.bfloat16)


def draw_tile_lists(key, part):
    key = jax.random.fold_in(key, 7)
    first_key, second_key = jax.random.split(key)
    tile_ids = jnp.arange(TILES)
    device = tile_ids // TILES_T
    time_pos = tile_ids % TILES_T
    height_pos = device // TILES_W
    width_pos = device % TILES_W
    offsets = jnp.arange(27)
    step_t = offsets // 9 - 1
    step_h = offsets // 3 % 3 - 1
    step_w = offsets % 3 - 1
    near_t = time_pos[:, None] + step_t[None, :]
    near_h = height_pos[:, None] + step_h[None, :]
    near_w = width_pos[:, None] + step_w[None, :]
    inside = (near_t >= 0) & (near_t < TILES_T) & (near_h >= 0) & (near_h < TILES_H) & (near_w >= 0) & (near_w < TILES_W)
    numbers = (near_h * TILES_W + near_w) * TILES_T + near_t
    noise = jax.random.randint(first_key, (TILES, 27), 0, 1 << 20)
    ranking = jnp.where(offsets[None, :] == 13, 1 << 30, jnp.where(inside, noise * 32 + offsets[None, :], -1 - offsets[None, :]))
    _, order = lax.top_k(ranking, NB)
    picked = jnp.take_along_axis(numbers, order, axis=1)
    count = jax.random.randint(second_key, (TILES,), max(2, NB // 2), NB + 1)
    special = (min(1, TILES_H - 1) * TILES_W + 1) * TILES_T + min(1, TILES_T - 1)
    count = jnp.where(tile_ids == special, NB, count)
    count = jnp.minimum(count, jnp.sum(inside, axis=1))
    slots = jnp.arange(NB)
    return jnp.where(slots[None, :] < count[:, None], picked, -1).astype(jnp.int32)


def shard_levels(own_key, dims, pieces, low, top_value):
    loudness = 1.0
    for position, blocks in pieces:
        heights = jax.random.uniform(jax.random.fold_in(jax.random.fold_in(own_key, 6), position), (blocks,), jnp.float32, low / len(pieces), top_value / len(pieces))
        loudness = loudness * jnp.repeat(jnp.exp(heights), dims[position] // blocks).reshape((-1,) + (1,) * (len(dims) - 1 - position))
    return loudness


def normal_values(stream_key, dims, spread, bound, cuts=(), kind=jnp.bfloat16):
    values = spread * jax.random.normal(stream_key, dims, jnp.float32)
    if cuts:
        values = values * shard_levels(stream_key, dims, cuts, -0.22, 0.18)
    return jnp.clip(values, -bound, bound).astype(kind)


def setup_inputs(seed: int = 0) -> dict:
    seeds = jax.random.split(jax.random.key(seed), 9)
    return {
        "q_video": draw_q_video(jax.random.fold_in(seeds[8], 71), 0),
        "k_video": draw_k_video(jax.random.fold_in(seeds[8], 71), 0),
        "v_video": normal_values(seeds[2], (VIDEO, FEATURES), 1.0, 6.0, ((0, 64), (1, 8))),
        "q_text": draw_q_text(jax.random.fold_in(seeds[8], 71), 0),
        "k_text": normal_values(seeds[4], (TEXT, FEATURES), 1.0, 6.0, ((0, 64), (1, 8))),
        "v_text": normal_values(seeds[5], (TEXT, FEATURES), 1.0, 6.0, ((0, 64), (1, 8))),
        "tile_lists": draw_tile_lists(jax.random.fold_in(seeds[8], 71), 0),
        "text_len": jax.random.randint(seeds[7], (1,), TEXT // 4, TEXT + 1).astype(jnp.int32),
    }


def attend(queries, keys, values, live, scale):
    scores = jnp.einsum('qhd,khd->hqk', queries.astype(jnp.float32), keys.astype(jnp.float32)) * scale
    scores = jnp.where(live[None, None, :], scores, -jnp.inf)
    peak = lax.optimization_barrier(jnp.max(scores, axis=-1, keepdims=True))
    unrounded = jnp.exp(scores - peak)
    total = lax.optimization_barrier(jnp.sum(unrounded, axis=-1))
    weights = lax.optimization_barrier(unrounded.astype(jnp.bfloat16)).astype(jnp.float32)
    summed = jnp.einsum('hqk,khd->qhd', weights, values.astype(jnp.float32))
    return (summed / jnp.transpose(total)[:, :, None]).astype(jnp.bfloat16)

def reference(q_video, k_video, v_video, q_text, k_text, v_text, tile_lists, text_len):
    scale = 1.0 / math.sqrt(HEAD_DIM)
    q_tiles = q_video.reshape(TILES, TILE_TOK, HEADS, HEAD_DIM)
    k_tiles = k_video.reshape(TILES, TILE_TOK, HEADS, HEAD_DIM)
    v_tiles = v_video.reshape(TILES, TILE_TOK, HEADS, HEAD_DIM)
    k_words = k_text.reshape(TEXT, HEADS, HEAD_DIM)
    v_words = v_text.reshape(TEXT, HEADS, HEAD_DIM)
    text_live = jnp.arange(TEXT).astype(jnp.int32) < text_len[0]

    def one_tile(index):
        listed = tile_lists[index]
        safe = jnp.maximum(listed, 0).astype(jnp.int32)
        keys = jnp.concatenate([k_tiles[safe].reshape(NB * TILE_TOK, HEADS, HEAD_DIM), k_words], 0)
        values = jnp.concatenate([v_tiles[safe].reshape(NB * TILE_TOK, HEADS, HEAD_DIM), v_words], 0)
        live = jnp.concatenate([jnp.repeat(listed >= 0, TILE_TOK), text_live])
        return attend(q_tiles[index], keys, values, live, scale)
    video_out = lax.map(one_tile, jnp.arange(TILES).astype(jnp.int32)).reshape(VIDEO, FEATURES)
    all_keys = jnp.concatenate([k_video.reshape(VIDEO, HEADS, HEAD_DIM), k_words], 0)
    all_values = jnp.concatenate([v_video.reshape(VIDEO, HEADS, HEAD_DIM), v_words], 0)
    all_live = jnp.concatenate([jnp.ones((VIDEO,), dtype=bool), text_live])
    head_queries = jnp.transpose(q_text.reshape(TEXT, HEADS, HEAD_DIM), (1, 0, 2))
    head_keys = jnp.transpose(all_keys, (1, 0, 2))
    head_values = jnp.transpose(all_values, (1, 0, 2))

    def one_head(triple):
        queries, keys, values = triple
        return attend(queries[:, None, :], keys[:, None, :], values[:, None, :], all_live, scale)[:, 0, :]
    per_head = lax.map(one_head, (head_queries, head_keys, head_values))
    text_out = jnp.transpose(per_head, (1, 0, 2)).reshape(TEXT, FEATURES)
    return (video_out, text_out)
```

```python
import functools
import math

import jax
import jax.numpy as jnp
import numpy as np
from jax import lax
from jax.experimental import pallas as pl
from jax.experimental.pallas import tpu as pltpu
from jax.sharding import Mesh
from jax.sharding import PartitionSpec as P


SIZES = (2, 8, 4, 4, 2)
NAMES = ("yl", "z", "x", "yh", "c")
GROUP = ("yl", "x", "c")
HEAD = 128
TILE = 384
ROWS = 2 * TILE
SLOTS = 8
BLOCK = 2 * ROWS + 16
PIECE = ROWS + 16
RATE = math.log2(math.e) / math.sqrt(HEAD)
VMEM = 40 * 1024 * 1024
CALLS = ((0, 1), (2,), (3,))
COST = pl.CostEstimate(flops=1 << 20, bytes_accessed=1 << 16, transcendentals=0)


def pairs_of(target):
    found = []
    for source in np.ndindex(*SIZES):
        aim = target(*source)
        if aim is not None:
            found.append(
                (int(np.ravel_multi_index(source, SIZES)), int(np.ravel_multi_index(aim, SIZES)))
            )
    return found


def send(value, target):
    return lax.ppermute(value, NAMES, pairs_of(target))


def to_column(turn):
    def target(yl, z, x, yh, c):
        i = (turn - z // 2) % 4
        return (yl, 3 * c + i, x, yh, z % 2) if i < 3 else None

    return target


def from_column(turn):
    def target(yl, z, x, yh, c):
        if z >= 6:
            return None
        r = (turn - z % 3) % 4
        return (yl, 2 * r + c, x, yh, z // 3)

    return target


def to_width(step):
    def target(yl, z, x, yh, c):
        width = 4 * c + x + step
        if z >= 6 or not 0 <= width < 8:
            return None
        return (yl, z, width % 4, yh, width // 4)

    return target


def across(yl, z, x, yh, c):
    return (1 - yl, z, x, yh, c) if z < 6 else None


def dot_nt(a, b):
    return lax.dot_general(a, b, (((1,), (1,)), ((), ())), preferred_element_type=jnp.float32)


def fold_lanes(op, block):
    out = block[:, :HEAD]
    for start in range(HEAD, block.shape[1], HEAD):
        out = op(out, block[:, start : start + HEAD])
    return out


def weights_of(scores, peak):
    parts = []
    for start in range(0, scores.shape[1], HEAD):
        parts.append(jnp.exp2((scores[:, start : start + HEAD] - peak) * RATE))
    return functools.reduce(jnp.add, parts), jnp.concatenate(parts, axis=1).astype(jnp.bfloat16)


def column_kernel(turns, params, lists, *refs):
    many = len(turns)
    queries, blocks, words = refs[:many], refs[many : many + 15], refs[many + 15]
    outs = refs[many + 16 : 2 * many + 16]
    pool, scores, sems = refs[2 * many + 16 :]
    copies, start = [], 0
    for n, block in enumerate(blocks):
        place = pl.ds(start, block.shape[0])
        copies.append(pltpu.make_async_copy(block, pool.at[place], sems.at[n]))
        start += block.shape[0]
    for copy in copies:
        copy.start()
    yl, width, head, text_len = params[0], params[1], params[2], params[3]
    for copy in copies:
        copy.wait()
    row = lax.broadcasted_iota(jnp.int32, (TILE, 256), 1)
    live = text_token(row) < text_len

    def key_row(entry):
        height = (entry >> 4) - yl * 4
        slot = jnp.where((height >= 0) & (height < 4), (height + head) & 3, 4)
        shift = ((entry >> 1) & 7) - width
        slot = slot + jnp.where(shift == 0, 0, jnp.where(shift < 0, 5, 10))
        return jnp.clip(slot, 0, 14) * BLOCK + (entry & 1) * TILE

    for spot, turn in enumerate(turns):
        found = []
        for half in range(2):
            base = (turn * 2 + half) * SLOTS
            rows, valid = [], []
            for j in range(SLOTS):
                entry = lists[base + j]
                valid.append(entry >= 0)
                rows.append(key_row(jnp.where(entry >= 0, entry, lists[base])))
            found.append((rows, valid))
        peaks = []
        for half, (rows, valid) in enumerate(found):
            q = queries[spot][half * TILE : (half + 1) * TILE, :]
            s = jnp.where(live, dot_nt(q, words[0]), -jnp.inf)
            scores[half, SLOTS, :, :256] = s
            peak = fold_lanes(jnp.maximum, s)
            for j in range(SLOTS):
                s = dot_nt(q, pool[pl.ds(pl.multiple_of(rows[j], 16), TILE), :])
                scores[half, j] = s
                s = fold_lanes(jnp.maximum, s)
                peak = jnp.maximum(peak, jnp.where(valid[j], s, -jnp.inf))
            peaks.append(jnp.max(peak, axis=1, keepdims=True))
        for half, (rows, valid) in enumerate(found):
            peak = jnp.broadcast_to(peaks[half], (TILE, HEAD))
            total, w = weights_of(scores[half, SLOTS, :, :256], peak)
            summed = jnp.dot(w, words[1], preferred_element_type=jnp.float32)
            for j in range(SLOTS):
                more, w = weights_of(scores[half, j], jnp.where(valid[j], peak, jnp.inf))
                total = total + more
                v = pool[pl.ds(pl.multiple_of(rows[j] + ROWS, 16), TILE), :]
                summed = summed + jnp.dot(w, v, preferred_element_type=jnp.float32)
            total = jnp.sum(total, axis=1, keepdims=True)
            outs[spot][half * TILE : (half + 1) * TILE, :] = (summed / total).astype(jnp.bfloat16)
        outs[spot][ROWS:, :] = jnp.zeros((PIECE - ROWS, HEAD), jnp.bfloat16)


def attend_column(turns, params, lists, queries, blocks, words):
    smem = pl.BlockSpec(memory_space=pltpu.SMEM)
    vmem = pl.BlockSpec(memory_space=pltpu.VMEM)
    hbm = pl.BlockSpec(memory_space=pl.ANY)
    count = len(turns)
    return pl.pallas_call(
        functools.partial(column_kernel, turns),
        out_shape=[jax.ShapeDtypeStruct((PIECE, HEAD), jnp.bfloat16)] * count,
        in_specs=[smem, smem] + [vmem] * count + [hbm] * 15 + [vmem],
        out_specs=[vmem] * count,
        scratch_shapes=[
            pltpu.VMEM((15 * BLOCK, HEAD), jnp.bfloat16),
            pltpu.VMEM((2, SLOTS + 1, TILE, TILE), jnp.float32),
            pltpu.SemaphoreType.DMA((15,)),
        ],
        compiler_params=pltpu.CompilerParams(vmem_limit_bytes=VMEM),
        cost_estimate=COST,
        name="attend_column",
    )(params, lists, *queries, *blocks, words)


def text_token(row):
    yl, x, z = row >> 7, (row >> 5) & 3, ((row >> 2) & 3) * 2 + ((row >> 4) & 1)
    return ((yl * 8 + z) * 4 + x) * 4 + (row & 3)


def stats_of(peak, total):
    lane = lax.broadcasted_iota(jnp.int32, (peak.shape[0], HEAD), 1)
    return jnp.where(lane == 0, peak, jnp.where(lane == 1, total, 0.0))


def text_kernel(limit, words, *refs):
    blocks, out = refs[:4], refs[4]
    row = lax.broadcasted_iota(jnp.int32, (256, 256), 1)
    q = words[0]
    scores = [dot_nt(q, block[:ROWS, :]) for block in blocks]
    scores.append(jnp.where(text_token(row) < limit[0], dot_nt(q, words[1]), -jnp.inf))
    values = [block[ROWS : 2 * ROWS, :] for block in blocks] + [words[2]]
    peak = functools.reduce(jnp.maximum, [fold_lanes(jnp.maximum, s) for s in scores])
    peak = jnp.max(peak, axis=1, keepdims=True)
    total, summed = 0.0, 0.0
    for s, v in zip(scores, values):
        more, w = weights_of(s, peak)
        total = total + more
        summed = summed + jnp.dot(w, v, preferred_element_type=jnp.float32)
    stats = stats_of(peak, jnp.sum(total, axis=1, keepdims=True))
    out[:, :HEAD] = summed
    out[:, HEAD:] = stats


def attend_text(limit, words, blocks):
    vmem = pl.BlockSpec(memory_space=pltpu.VMEM)
    return pl.pallas_call(
        text_kernel,
        out_shape=jax.ShapeDtypeStruct((256, 256), jnp.float32),
        in_specs=[pl.BlockSpec(memory_space=pltpu.SMEM)] + [vmem] * 5,
        out_specs=vmem,
        compiler_params=pltpu.CompilerParams(vmem_limit_bytes=VMEM),
        cost_estimate=COST,
        name="attend_text",
    )(limit, words, *blocks)


def merge_kernel(parts, out):
    peak = functools.reduce(jnp.maximum, [parts[n, :, 128:129] for n in range(16)])
    total, summed = 0.0, 0.0
    for n in range(16):
        scale = jnp.exp2((parts[n, :, 128:129] - peak) * RATE)
        total = total + parts[n, :, 129:130] * scale
        summed = summed + parts[n, :, :HEAD] * scale
    out[...] = (summed / total).astype(jnp.bfloat16)


def merge_text(parts):
    vmem = pl.BlockSpec(memory_space=pltpu.VMEM)
    return pl.pallas_call(
        merge_kernel,
        out_shape=jax.ShapeDtypeStruct((16, HEAD), jnp.bfloat16),
        in_specs=[vmem],
        out_specs=vmem,
        name="merge_text",
    )(parts)


def after(value, *others):
    return lax.optimization_barrier((value, *others))[0]


def shards(q_video, k_video, v_video, q_text, k_text, v_text, tile_lists, text_len):
    yl, z, x, c = (lax.axis_index(name) for name in ("yl", "z", "x", "c"))
    r, head = z // 2, z % 3

    def head_of(array, turn):
        i = jnp.minimum((turn - r) % 4, 2)
        return lax.dynamic_slice(array, (0, i * HEAD), (array.shape[0], HEAD))

    text = jnp.concatenate([q_text, k_text, v_text, jnp.zeros_like(q_text)], axis=0)
    listed = jnp.pad(tile_lists.astype(jnp.bfloat16).reshape(1, 16), ((0, 15), (0, 112)))
    own, queries, left, right = {}, {}, {}, {}
    for turn, behind in ((0, None), (2, None), (1, 0), (3, 2)):
        block = [head_of(array, turn) for array in (k_video, v_video, text)]
        block = jnp.concatenate(block, axis=0)
        if behind is not None:
            block = after(block, own[behind])
        own[turn] = send(block, to_column(turn))
    own[4] = send(
        lax.select_n((jnp.where(yl == 0, 3, 0) + head) % 4, *(own[turn] for turn in range(4))),
        across,
    )
    for turn, behind in ((0, None), (2, None), (1, 0), (3, 2), (4, 1)):
        block = own[turn] if behind is None else after(own[turn], left[behind], right[behind])
        left[turn] = send(block, to_width(1))
        right[turn] = send(block, to_width(-1))
    for turn, behind in ((0, own[1]), (2, own[3]), (1, left[2]), (3, left[1])):
        piece = jnp.concatenate([head_of(q_video, turn), listed], axis=0)
        queries[turn] = send(after(piece, behind), to_column(turn))
    own, left, right = ([group[n] for n in range(5)] for group in (own, left, right))
    blocks = own + left + right

    held = jnp.stack([block[2 * ROWS :] for block in own[:4]])
    held = lax.dynamic_slice(jnp.concatenate([held, held]), (head, 0, 0), (4, 12, HEAD))
    held = held.reshape(4, 3, 4, HEAD).transpose(1, 0, 2, 3).reshape(3, 16, HEAD)
    held = after(held, left[0], right[0], left[2], right[2])
    held = lax.all_to_all(jnp.broadcast_to(held, (16, 3, 16, HEAD)), GROUP, 0, 0, tiled=True)
    held = held.transpose(1, 0, 2, 3).reshape(3, 256, HEAD)

    first_column = (yl == 0) & (x == 0) & (c == 0)
    limit = jnp.where(first_column, text_len[0], 0).astype(jnp.int32)[None]
    held = after(held, left[1], right[1], left[3], right[3], queries[0], queries[2])
    packed = after(attend_text(limit, held, own[:4]), left[4], right[4], queries[1], queries[3])
    packed = lax.all_to_all(packed.reshape(16, 16, 256), GROUP, 0, 0, tiled=True)
    text_done = merge_text(packed)

    lists = jnp.stack([queries[turn][ROWS, :16] for turn in range(4)]).astype(jnp.int32).reshape(64)
    params = jnp.stack([yl, 4 * c + x, head, text_len[0]]).astype(jnp.int32)
    back = []
    for turns in CALLS:
        some = [queries[turn] for turn in turns]
        if back:
            some[0] = after(some[0], *(back[:2] if len(back) > 2 else [text_done]))
        done = attend_column(turns, params, lists, some, blocks, held[1:])
        for turn, piece in zip(turns, done):
            mine = lax.dynamic_slice(text_done, ((turn - head) % 4 * 4, 0), (4, HEAD))
            piece = lax.dynamic_update_slice(piece, jnp.pad(mine, ((0, 12), (0, 0))), (ROWS, 0))
            back.append(send(piece, from_column(turn)))
    heads = [lax.select_n((r + i) % 4, *back) for i in range(3)]
    out = jnp.concatenate(heads, axis=1)
    video_out = lax.all_to_all(out[:ROWS], ("yh", "c"), split_axis=0, concat_axis=1, tiled=True)
    return (video_out, out[ROWS : ROWS + 4])


def solution(mesh):
    fine = Mesh(mesh.devices.reshape(SIZES), NAMES)
    tile, head = ("yl", "z", "x"), ("yh", "c")
    split = P(tile, head)
    in_specs = (split,) * 6 + (P(tile, None), P())
    out_specs = (P(tile + head, None), split)
    return jax.shard_map(shards, mesh=fine, in_specs=in_specs, out_specs=out_specs, check_vma=False)
```

```python
import functools
import math

import jax
import jax.numpy as jnp
import numpy as np
from jax import lax
from jax.experimental import pallas as pl
from jax.experimental.pallas import tpu as pltpu
from jax.sharding import Mesh
from jax.sharding import PartitionSpec as P


SIZES = (2, 8, 4, 4, 2)
NAMES = ("yl", "zr", "zp", "x", "yh", "c")
GROUP = ("yl", "x", "c")
HEAD = 128
TILE = 384
ROWS = 2 * TILE
SLOTS = 8
SHARE = ROWS // 8
CHUNK = SHARE + 16
BLOCK = 2 * ROWS + 16
RATE = math.log2(math.e) / math.sqrt(HEAD)
VMEM = 60 * 1024 * 1024
COST = pl.CostEstimate(flops=1 << 20, bytes_accessed=1 << 16, transcendentals=0)


def pairs_of(target):
    found = []
    for source in np.ndindex(*SIZES):
        aim = target(*source)
        if aim is not None:
            found.append(
                (int(np.ravel_multi_index(source, SIZES)), int(np.ravel_multi_index(aim, SIZES)))
            )
    return found


def send(value, target):
    return lax.ppermute(value, NAMES, pairs_of(target))


def to_column(turn):
    def target(yl, z, x, yh, c):
        i = (turn - z // 2) % 4
        return (yl, 4 * c + i, x, yh, z % 2) if i < 3 else None

    return target


def to_width(step):
    def target(yl, z, x, yh, c):
        width = 4 * c + x + step
        if z % 4 == 3 or not 0 <= width < 8:
            return None
        return (yl, z, width % 4, yh, width // 4)

    return target


def across(yl, z, x, yh, c):
    return (1 - yl, z, x, yh, c) if z % 4 < 3 else None


def dot_nt(a, b):
    return lax.dot_general(a, b, (((1,), (1,)), ((), ())), preferred_element_type=jnp.float32)


def fold_lanes(op, block):
    out = block[:, :HEAD]
    for start in range(HEAD, block.shape[1], HEAD):
        out = op(out, block[:, start : start + HEAD])
    return out


def weights_of(scores, peak):
    parts = []
    for start in range(0, scores.shape[1], HEAD):
        parts.append(jnp.exp2((scores[:, start : start + HEAD] - peak) * RATE))
    return functools.reduce(jnp.add, parts), jnp.concatenate(parts, axis=1).astype(jnp.bfloat16)


def column_kernel(params, lists, *refs):
    queries, blocks, (words, parts, out, pool, scores, sems) = refs[:4], refs[4:16], refs[16:]
    copies, start = [], 0
    for n, block in enumerate(blocks):
        place = pl.ds(start, block.shape[0])
        copies.append(pltpu.make_async_copy(block, pool.at[place], sems.at[n]))
        start += block.shape[0]
    for copy in copies:
        copy.start()
    yl, width, head, text_len = params[0], params[1], params[2], params[3]
    for copy in copies:
        copy.wait()
    row = lax.broadcasted_iota(jnp.int32, (TILE, 256), 1)
    live = text_token(row) < text_len

    def key_row(entry):
        height = (entry >> 4) - yl * 4
        turn = height + head
        slot = (turn & 1) * 2 + ((turn >> 1) & 1)
        slot = jnp.where((height >= 0) & (height < 4), slot, 4)
        shift = ((entry >> 1) & 7) - width
        slot = slot + jnp.where(shift == 0, 0, jnp.where(shift < 0, 5, 10))
        return jnp.clip(slot, 0, 14) * BLOCK + (entry & 1) * TILE

    text = merge_text(parts)
    for n in range(4):
        for yh in range(4):
            for c in range(2):
                out[c, n, yh, SHARE:, :] = text
    for turn in range(4):
        r = (turn - head) & 3
        found = []
        for half in range(2):
            base = (turn * 2 + half) * SLOTS
            rows, valid = [], []
            for j in range(SLOTS):
                entry = lists[base + j]
                valid.append(entry >= 0)
                rows.append(key_row(jnp.where(entry >= 0, entry, lists[base])))
            found.append((rows, valid))
        peaks = []
        for half, (rows, valid) in enumerate(found):
            q = queries[turn][half * TILE : (half + 1) * TILE, :]
            s = jnp.where(live, dot_nt(q, words[0]), -jnp.inf)
            scores[half, SLOTS, :, :256] = s
            peak = fold_lanes(jnp.maximum, s)
            for j in range(SLOTS):
                s = dot_nt(q, pool[pl.ds(pl.multiple_of(rows[j], 16), TILE), :])
                scores[half, j] = s
                s = fold_lanes(jnp.maximum, s)
                peak = jnp.maximum(peak, jnp.where(valid[j], s, -jnp.inf))
            peaks.append(jnp.max(peak, axis=1, keepdims=True))
        for half, (rows, valid) in enumerate(found):
            peak = jnp.broadcast_to(peaks[half], (TILE, HEAD))
            total, w = weights_of(scores[half, SLOTS, :, :256], peak)
            summed = jnp.dot(w, words[1], preferred_element_type=jnp.float32)
            for j in range(SLOTS):
                more, w = weights_of(scores[half, j], jnp.where(valid[j], peak, jnp.inf))
                total = total + more
                v = pool[pl.ds(pl.multiple_of(rows[j] + ROWS, 16), TILE), :]
                summed = summed + jnp.dot(w, v, preferred_element_type=jnp.float32)
            total = jnp.sum(total, axis=1, keepdims=True)
            done = (summed / total).astype(jnp.bfloat16)
            for n in range(4):
                out[n % 2, r, half * 2 + n // 2, :SHARE, :] = done[n * SHARE : (n + 1) * SHARE, :]


def attend_column(params, lists, queries, blocks, words, parts):
    smem = pl.BlockSpec(memory_space=pltpu.SMEM)
    vmem = pl.BlockSpec(memory_space=pltpu.VMEM)
    hbm = pl.BlockSpec(memory_space=pl.ANY)
    return pl.pallas_call(
        column_kernel,
        out_shape=jax.ShapeDtypeStruct((2, 4, 4, CHUNK, HEAD), jnp.bfloat16),
        in_specs=[smem, smem] + [vmem] * 4 + [hbm] * 12 + [vmem] * 2,
        out_specs=vmem,
        scratch_shapes=[
            pltpu.VMEM((15 * BLOCK, HEAD), jnp.bfloat16),
            pltpu.VMEM((2, SLOTS + 1, TILE, TILE), jnp.float32),
            pltpu.SemaphoreType.DMA((12,)),
        ],
        compiler_params=pltpu.CompilerParams(vmem_limit_bytes=VMEM),
        cost_estimate=COST,
        name="attend_column",
    )(params, lists, *queries, *blocks, words, parts)


def text_token(row):
    yl, x, z = row >> 7, (row >> 5) & 3, ((row >> 2) & 3) * 2 + ((row >> 4) & 1)
    return ((yl * 8 + z) * 4 + x) * 4 + (row & 3)


def stats_of(peak, total):
    lane = lax.broadcasted_iota(jnp.int32, (peak.shape[0], HEAD), 1)
    return jnp.where(lane == 0, peak, jnp.where(lane == 1, total, 0.0))


def text_kernel(limit, words, *refs):
    blocks, out = refs[:3], refs[3]
    row = lax.broadcasted_iota(jnp.int32, (256, 256), 1)
    q = words[0]
    scores, values = [], []
    for block in blocks:
        for start in range(0, block.shape[0], BLOCK):
            scores.append(dot_nt(q, block[start : start + ROWS, :]))
            values.append(block[start + ROWS : start + 2 * ROWS, :])
    scores.append(jnp.where(text_token(row) < limit[0], dot_nt(q, words[1]), -jnp.inf))
    values.append(words[2])
    peak = functools.reduce(jnp.maximum, [fold_lanes(jnp.maximum, s) for s in scores])
    peak = jnp.max(peak, axis=1, keepdims=True)
    total, summed = 0.0, 0.0
    for s, v in zip(scores, values):
        more, w = weights_of(s, peak)
        total = total + more
        summed = summed + jnp.dot(w, v, preferred_element_type=jnp.float32)
    stats = stats_of(peak, jnp.sum(total, axis=1, keepdims=True))
    out[:, :HEAD] = summed
    out[:, HEAD:] = stats


def attend_text(limit, words, blocks):
    vmem = pl.BlockSpec(memory_space=pltpu.VMEM)
    return pl.pallas_call(
        text_kernel,
        out_shape=jax.ShapeDtypeStruct((256, 256), jnp.float32),
        in_specs=[pl.BlockSpec(memory_space=pltpu.SMEM)] + [vmem] * 4,
        out_specs=vmem,
        compiler_params=pltpu.CompilerParams(vmem_limit_bytes=VMEM),
        cost_estimate=COST,
        name="attend_text",
    )(limit, words, *blocks)


def merge_text(parts):
    peak = functools.reduce(jnp.maximum, [parts[n, :, 128:129] for n in range(16)])
    total, summed = 0.0, 0.0
    for n in range(16):
        scale = jnp.exp2((parts[n, :, 128:129] - peak) * RATE)
        total = total + parts[n, :, 129:130] * scale
        summed = summed + parts[n, :, :HEAD] * scale
    return (summed / total).astype(jnp.bfloat16)


def after(value, *others):
    return lax.optimization_barrier((value, *others))[0]


def shards(q_video, k_video, v_video, q_text, k_text, v_text, tile_lists, text_len):
    yl, r, p, x, c = (lax.axis_index(name) for name in ("yl", "zr", "zp", "x", "c"))
    z = 2 * r + p
    head = z % 4

    def head_of(array, turn):
        i = jnp.minimum((turn - r) % 4, 2)
        return lax.dynamic_slice(array, (0, i * HEAD), (array.shape[0], HEAD))

    listed = jnp.pad(tile_lists.astype(jnp.bfloat16).reshape(1, 16), ((0, 3), (0, 112)))
    text = jnp.concatenate([q_text, k_text, v_text, jnp.tile(listed, (1, 3))], axis=0)
    own = {}
    for turn, behind in ((0, None), (2, None), (1, 0), (3, 2)):
        block = [head_of(array, turn) for array in (k_video, v_video, text)]
        block = jnp.concatenate(block, axis=0)
        if behind is not None:
            block = after(block, own[behind])
        own[turn] = send(block, to_column(turn))
    left, right = {}, {}
    for turn in (0, 2):
        left[turn], right[turn] = send(own[turn], to_width(1)), send(own[turn], to_width(-1))

    held = jnp.stack([own[turn][2 * ROWS :] for turn in range(4)])
    lists = held[:, 12, :16].astype(jnp.int32).reshape(64)
    held = lax.dynamic_slice(jnp.concatenate([held, held]), (head, 0, 0), (4, 12, HEAD))
    held = held.reshape(4, 3, 4, HEAD).transpose(1, 0, 2, 3).reshape(3, 16, HEAD)
    held = after(held, left[0], right[0], left[2], right[2])
    held = lax.all_to_all(jnp.broadcast_to(held, (16, 3, 16, HEAD)), GROUP, 0, 0, tiled=True)
    held = held.transpose(1, 0, 2, 3).reshape(3, 256, HEAD)

    edge = lax.select_n((jnp.where(yl == 0, 3, 0) + head) % 4, *(own[turn] for turn in range(4)))
    own[4] = send(edge, across)
    both = jnp.concatenate([own[1], own[3]], axis=0)
    left[1], right[1] = send(both, to_width(1)), send(both, to_width(-1))
    marks = (left[2], held, left[2], held)
    queries = [
        send(after(head_of(q_video, turn), mark), to_column(turn)) for turn, mark in enumerate(marks)
    ]

    first_column = (yl == 0) & (x == 0) & (c == 0)
    limit = jnp.where(first_column, text_len[0], 0).astype(jnp.int32)[None]
    held = after(held, queries[0], queries[2])
    packed = attend_text(limit, held, [own[0], own[2], both])
    edges = after(own[4], left[1], right[1])
    left[4], right[4] = send(edges, to_width(1)), send(edges, to_width(-1))
    packed = lax.all_to_all(packed.reshape(16, 16, 256), GROUP, 0, 0, tiled=True)

    blocks = [own[0], own[2], both, own[4], left[0], left[2], left[1], left[4]]
    blocks += [right[0], right[2], right[1], right[4]]

    params = jnp.stack([yl, 4 * c + x, head, text_len[0]]).astype(jnp.int32)
    done = attend_column(params, lists, queries, blocks, held[1:], packed)
    done = lax.all_to_all(done, "c", 0, 0, tiled=True)
    done = lax.all_to_all(done.reshape(32, CHUNK, HEAD), ("zp", "zr", "yh"), 0, 0, tiled=True)
    done = done.reshape(2, 4, 4, CHUNK, HEAD).transpose(3, 2, 1, 0, 4).reshape(CHUNK, 4, 2, 4, HEAD)
    video_out = done[:SHARE, :, :, :3].reshape(SHARE, 24 * HEAD)
    yh = lax.axis_index("yh")
    text_out = lax.dynamic_slice(done, (SHARE + 4 * r, yh, c, 0, 0), (4, 1, 1, 3, HEAD))
    return (video_out, text_out.reshape(4, 3 * HEAD))


def solution(mesh):
    fine = Mesh(mesh.devices.reshape(2, 4, 2, 4, 4, 2), NAMES)
    tile, head = ("yl", "zr", "zp", "x"), ("yh", "c")
    split = P(tile, head)
    in_specs = (split,) * 6 + (P(tile, None), P())
    out_specs = (P(tile + head, None), split)
    return jax.shard_map(shards, mesh=fine, in_specs=in_specs, out_specs=out_specs, check_vma=False)
```

```python
import functools
import math

import jax
import jax.numpy as jnp
import numpy as np
from jax import lax
from jax.experimental import pallas as pl
from jax.experimental.pallas import tpu as pltpu
from jax.sharding import Mesh
from jax.sharding import PartitionSpec as P


SIZES = (2, 8, 4, 4, 2)
NAMES = ("yl", "zr", "zp", "x", "yh", "c")
GROUP = ("yl", "x", "c")
HEAD = 128
TILE = 384
ROWS = 2 * TILE
SLOTS = 8
SHARE = ROWS // 8
CHUNK = SHARE + 16
BLOCK = 2 * ROWS + 16
RATE = math.log2(math.e) / math.sqrt(HEAD)
VMEM = 60 * 1024 * 1024
COST = pl.CostEstimate(flops=1 << 20, bytes_accessed=1 << 16, transcendentals=0)


def pairs_of(target):
    found = []
    for source in np.ndindex(*SIZES):
        aim = target(*source)
        if aim is not None:
            found.append(
                (int(np.ravel_multi_index(source, SIZES)), int(np.ravel_multi_index(aim, SIZES)))
            )
    return found


def send(value, target):
    return lax.ppermute(value, NAMES, pairs_of(target))


def to_column(turn):
    def target(yl, z, x, yh, c):
        i = (turn - z // 2) % 4
        return (yl, 4 * c + i, x, yh, z % 2) if i < 3 else None

    return target


def to_width(step):
    def target(yl, z, x, yh, c):
        width = 4 * c + x + step
        if z % 4 == 3 or not 0 <= width < 8:
            return None
        return (yl, z, width % 4, yh, width // 4)

    return target


def across(yl, z, x, yh, c):
    return (1 - yl, z, x, yh, c) if z % 4 < 3 else None


def dot_nt(a, b):
    return lax.dot_general(a, b, (((1,), (1,)), ((), ())), preferred_element_type=jnp.float32)


def fold_lanes(op, block):
    out = block[:, :HEAD]
    for start in range(HEAD, block.shape[1], HEAD):
        out = op(out, block[:, start : start + HEAD])
    return out


def weights_of(scores, peak):
    parts = []
    for start in range(0, scores.shape[1], HEAD):
        parts.append(jnp.exp2((scores[:, start : start + HEAD] - peak) * RATE))
    return functools.reduce(jnp.add, parts), jnp.concatenate(parts, axis=1).astype(jnp.bfloat16)


def column_kernel(params, lists, *refs):
    queries, blocks, (words, parts, out, pool, scores, sems) = refs[:4], refs[4:16], refs[16:]
    copies, start = [], 0
    for n, block in enumerate(blocks):
        place = pl.ds(start, block.shape[0])
        copies.append(pltpu.make_async_copy(block, pool.at[place], sems.at[n]))
        start += block.shape[0]
    for copy in copies:
        copy.start()
    yl, width, head, text_len = params[0], params[1], params[2], params[3]
    for copy in copies:
        copy.wait()
    row = lax.broadcasted_iota(jnp.int32, (TILE, 256), 1)
    live = text_token(row) < text_len

    def key_row(entry):
        height = (entry >> 4) - yl * 4
        turn = height + head
        slot = (turn & 1) * 2 + ((turn >> 1) & 1)
        slot = jnp.where((height >= 0) & (height < 4), slot, 4)
        shift = ((entry >> 1) & 7) - width
        slot = slot + jnp.where(shift == 0, 0, jnp.where(shift < 0, 5, 10))
        return jnp.clip(slot, 0, 14) * BLOCK + (entry & 1) * TILE

    text = merge_text(parts)
    for n in range(4):
        for yh in range(4):
            for c in range(2):
                out[c, n, yh, SHARE:, :] = text
    for turn in range(4):
        r = (turn - head) & 3
        found = []
        for half in range(2):
            base = (turn * 2 + half) * SLOTS
            rows, valid = [], []
            for j in range(SLOTS):
                entry = lists[base + j]
                valid.append(entry >= 0)
                rows.append(key_row(jnp.where(entry >= 0, entry, lists[base])))
            found.append((rows, valid))
        peaks = []
        for half, (rows, valid) in enumerate(found):
            q = queries[turn][half * TILE : (half + 1) * TILE, :]
            s = jnp.where(live, dot_nt(q, words[0]), -jnp.inf)
            scores[half, SLOTS, :, :256] = s
            peak = fold_lanes(jnp.maximum, s)
            for j in range(SLOTS):
                s = dot_nt(q, pool[pl.ds(pl.multiple_of(rows[j], 16), TILE), :])
                scores[half, j] = s
                s = fold_lanes(jnp.maximum, s)
                peak = jnp.maximum(peak, jnp.where(valid[j], s, -jnp.inf))
            peaks.append(jnp.max(peak, axis=1, keepdims=True))
        for half, (rows, valid) in enumerate(found):
            peak = jnp.broadcast_to(peaks[half], (TILE, HEAD))
            total, w = weights_of(scores[half, SLOTS, :, :256], peak)
            summed = jnp.dot(w, words[1], preferred_element_type=jnp.float32)
            for j in range(SLOTS):
                more, w = weights_of(scores[half, j], jnp.where(valid[j], peak, jnp.inf))
                total = total + more
                v = pool[pl.ds(pl.multiple_of(rows[j] + ROWS, 16), TILE), :]
                summed = summed + jnp.dot(w, v, preferred_element_type=jnp.float32)
            total = jnp.sum(total, axis=1, keepdims=True)
            done = (summed / total).astype(jnp.bfloat16)
            for n in range(4):
                out[n % 2, r, half * 2 + n // 2, :SHARE, :] = done[n * SHARE : (n + 1) * SHARE, :]


def attend_column(params, lists, queries, blocks, words, parts):
    smem = pl.BlockSpec(memory_space=pltpu.SMEM)
    vmem = pl.BlockSpec(memory_space=pltpu.VMEM)
    hbm = pl.BlockSpec(memory_space=pl.ANY)
    return pl.pallas_call(
        column_kernel,
        out_shape=jax.ShapeDtypeStruct((2, 4, 4, CHUNK, HEAD), jnp.bfloat16),
        in_specs=[smem, smem] + [vmem] * 4 + [hbm] * 12 + [vmem] * 2,
        out_specs=vmem,
        scratch_shapes=[
            pltpu.VMEM((15 * BLOCK, HEAD), jnp.bfloat16),
            pltpu.VMEM((2, SLOTS + 1, TILE, TILE), jnp.float32),
            pltpu.SemaphoreType.DMA((12,)),
        ],
        compiler_params=pltpu.CompilerParams(vmem_limit_bytes=VMEM),
        cost_estimate=COST,
        name="attend_column",
    )(params, lists, *queries, *blocks, words, parts)


def text_token(row):
    yl, x, z = row >> 7, (row >> 5) & 3, ((row >> 2) & 3) * 2 + ((row >> 4) & 1)
    return ((yl * 8 + z) * 4 + x) * 4 + (row & 3)


def stats_of(peak, total):
    lane = lax.broadcasted_iota(jnp.int32, (peak.shape[0], HEAD), 1)
    return jnp.where(lane == 0, peak, jnp.where(lane == 1, total, 0.0))


def text_kernel(limit, words, *refs):
    blocks, out = refs[:3], refs[3]
    row = lax.broadcasted_iota(jnp.int32, (256, 256), 1)
    q = words[0]
    scores, values = [], []
    for block in blocks:
        for start in range(0, block.shape[0], BLOCK):
            scores.append(dot_nt(q, block[start : start + ROWS, :]))
            values.append(block[start + ROWS : start + 2 * ROWS, :])
    scores.append(jnp.where(text_token(row) < limit[0], dot_nt(q, words[1]), -jnp.inf))
    values.append(words[2])
    peak = functools.reduce(jnp.maximum, [fold_lanes(jnp.maximum, s) for s in scores])
    peak = jnp.max(peak, axis=1, keepdims=True)
    total, summed = 0.0, 0.0
    for s, v in zip(scores, values):
        more, w = weights_of(s, peak)
        total = total + more
        summed = summed + jnp.dot(w, v, preferred_element_type=jnp.float32)
    stats = stats_of(peak, jnp.sum(total, axis=1, keepdims=True))
    out[:, :HEAD] = summed
    out[:, HEAD:] = stats


def attend_text(limit, words, blocks):
    vmem = pl.BlockSpec(memory_space=pltpu.VMEM)
    return pl.pallas_call(
        text_kernel,
        out_shape=jax.ShapeDtypeStruct((256, 256), jnp.float32),
        in_specs=[pl.BlockSpec(memory_space=pltpu.SMEM)] + [vmem] * 4,
        out_specs=vmem,
        compiler_params=pltpu.CompilerParams(vmem_limit_bytes=VMEM),
        cost_estimate=COST,
        name="attend_text",
    )(limit, words, *blocks)


def merge_text(parts):
    peak = functools.reduce(jnp.maximum, [parts[n, :, 128:129] for n in range(16)])
    total, summed = 0.0, 0.0
    for n in range(16):
        scale = jnp.exp2((parts[n, :, 128:129] - peak) * RATE)
        total = total + parts[n, :, 129:130] * scale
        summed = summed + parts[n, :, :HEAD] * scale
    return (summed / total).astype(jnp.bfloat16)


def after(value, *others):
    return lax.optimization_barrier((value, *others))[0]


def shards(q_video, k_video, v_video, q_text, k_text, v_text, tile_lists, text_len):
    yl, r, p, x, c = (lax.axis_index(name) for name in ("yl", "zr", "zp", "x", "c"))
    z = 2 * r + p
    head = z % 4

    def head_of(array, turn):
        i = jnp.minimum((turn - r) % 4, 2)
        return lax.dynamic_slice(array, (0, i * HEAD), (array.shape[0], HEAD))

    listed = jnp.pad(tile_lists.astype(jnp.bfloat16).reshape(1, 16), ((0, 3), (0, 112)))
    text = jnp.concatenate([q_text, k_text, v_text, jnp.tile(listed, (1, 3))], axis=0)
    own = {}
    for turn, behind in ((0, None), (2, None), (1, 0), (3, 2)):
        block = [head_of(array, turn) for array in (k_video, v_video, text)]
        block = jnp.concatenate(block, axis=0)
        if behind is not None:
            block = after(block, own[behind])
        own[turn] = send(block, to_column(turn))
    left, right = {}, {}
    for turn in (0, 2):
        left[turn], right[turn] = send(own[turn], to_width(1)), send(own[turn], to_width(-1))

    held = jnp.stack([own[turn][2 * ROWS :] for turn in range(4)])
    lists = held[:, 12, :16].astype(jnp.int32).reshape(64)
    held = lax.dynamic_slice(jnp.concatenate([held, held]), (head, 0, 0), (4, 12, HEAD))
    held = held.reshape(4, 3, 4, HEAD).transpose(1, 0, 2, 3).reshape(3, 16, HEAD)
    held = after(held, left[0], right[0], left[2], right[2])
    held = lax.all_to_all(jnp.broadcast_to(held, (16, 3, 16, HEAD)), GROUP, 0, 0, tiled=True)
    held = held.transpose(1, 0, 2, 3).reshape(3, 256, HEAD)

    edge = lax.select_n((jnp.where(yl == 0, 3, 0) + head) % 4, *(own[turn] for turn in range(4)))
    own[4] = send(edge, across)
    both = jnp.concatenate([own[1], own[3]], axis=0)
    left[1], right[1] = send(both, to_width(1)), send(both, to_width(-1))
    marks = (left[2], held, left[2], held)
    queries = [
        send(after(head_of(q_video, turn), mark), to_column(turn)) for turn, mark in enumerate(marks)
    ]

    first_column = (yl == 0) & (x == 0) & (c == 0)
    limit = jnp.where(first_column, text_len[0], 0).astype(jnp.int32)[None]
    held = after(held, queries[0], queries[2])
    packed = attend_text(limit, held, [own[0], own[2], both])
    edges = after(own[4], left[1], right[1], queries[1], queries[3])
    left[4], right[4] = send(edges, to_width(1)), send(edges, to_width(-1))
    packed = lax.all_to_all(packed.reshape(16, 16, 256), GROUP, 0, 0, tiled=True)

    blocks = [own[0], own[2], both, own[4], left[0], left[2], left[1], left[4]]
    blocks += [right[0], right[2], right[1], right[4]]

    params = jnp.stack([yl, 4 * c + x, head, text_len[0]]).astype(jnp.int32)
    done = attend_column(params, lists, queries, blocks, held[1:], packed)
    done = lax.all_to_all(done, "c", 0, 0, tiled=True)
    done = lax.all_to_all(done.reshape(32, CHUNK, HEAD), ("zp", "zr", "yh"), 0, 0, tiled=True)
    done = done.reshape(2, 4, 4, CHUNK, HEAD).transpose(3, 2, 1, 0, 4).reshape(CHUNK, 4, 2, 4, HEAD)
    video_out = done[:SHARE, :, :, :3].reshape(SHARE, 24 * HEAD)
    yh = lax.axis_index("yh")
    text_out = lax.dynamic_slice(done, (SHARE + 4 * r, yh, c, 0, 0), (4, 1, 1, 3, HEAD))
    return (video_out, text_out.reshape(4, 3 * HEAD))


def solution(mesh):
    fine = Mesh(mesh.devices.reshape(2, 4, 2, 4, 4, 2), NAMES)
    tile, head = ("yl", "zr", "zp", "x"), ("yh", "c")
    split = P(tile, head)
    in_specs = (split,) * 6 + (P(tile, None), P())
    out_specs = (P(tile + head, None), split)
    return jax.shard_map(shards, mesh=fine, in_specs=in_specs, out_specs=out_specs, check_vma=False)
```
